128 devices in a mesh: inp: 8 (over y, z_hi), tm: 16 (over x, z_lo, core).
Axes of the slice: x: 4, y: 4, z: 4 (z_hi: 2, z_lo: 2; z = z_hi * 2 + z_lo), core: 2. Of those that a mesh axis runs over, the one named last changes fastest.
Arguments:
- volt: bfloat16 [512, 573440], P('inp', 'tm'), may hold values from -800 to 800
Outputs:
- visibility: float32 [512, 2, 512, 512], P(('inp', 'tm'))
The draws below stay inside these ranges and needn't reach their ends.
All inputs are finite; a program needn't handle non-finite values.
Results may differ from the reference program's by a relative error of at most 0.0013.
Values may be sent and summed in bfloat16 or wider, within the bound.
A program may use at most 128 MiB of HBM per device.

```python
import math
import jax
import jax.numpy as jnp
from jax import lax

NI = 512
FRAME = 1024
TAPS = 4
FR_DEV = 32
CH = 512
F = 512
SAMP = 573440
N_TM = 16


def draw_volt(key, part):
    key = jax.random.fold_in(key, 11)
    key_noise, key_common, key_gain = jax.random.split(key, 3)
    position = jnp.arange(SAMP, dtype=jnp.float32) / SAMP
    noise = jax.random.truncated_normal(key_noise, -4.0, 4.0, (NI, SAMP), jnp.float32)
    common = jax.random.truncated_normal(key_common, -4.0, 4.0, (SAMP,), jnp.float32)
    gains = jnp.exp(jax.random.uniform(key_gain, (NI, 1), jnp.float32, 0.0, math.log(10.0)))
    envelope = jnp.exp(math.log(3.0) * position)
    signal = (noise + 0.7 * common[None, :]) * gains * envelope[None, :]
    return signal.astype(jnp.bfloat16)


def setup_inputs(seed: int = 0) -> dict:
    keys = jax.random.split(jax.random.key(seed), 2)
    volt = draw_volt(jax.random.fold_in(keys[1], 71), 0)
    return dict(volt=volt)


def pfb_window(taps, frame):
    span = taps * frame
    index = jnp.arange(span, dtype=jnp.float32)
    shifted = (index - span / 2 + 0.5) / frame
    shaped = jnp.sinc(shifted) * (0.54 - 0.46 * jnp.cos(2.0 * jnp.pi * index / (span - 1)))
    return shaped.reshape(taps, frame)

def twiddles(frame):
    chans = frame // 2
    column = jnp.arange(chans, dtype=jnp.int32)[:, None]
    sample = jnp.arange(frame, dtype=jnp.int32)[None, :]
    phase = (column * sample % frame).astype(jnp.float32) * (2.0 * jnp.pi / frame)
    return jnp.stack([jnp.cos(phase), -jnp.sin(phase)], axis=1).astype(jnp.bfloat16)

def reference(volt):
    segments = volt.reshape(NI, N_TM, FR_DEV + TAPS - 1, FRAME)
    window = pfb_window(TAPS, FRAME)
    table = twiddles(FRAME).astype(jnp.float32)

    def channelize(segment_id):
        piece = segments[:, segment_id].astype(jnp.float32)
        filtered = window[0][None, None, :] * piece[:, 0:FR_DEV]
        for tap in range(1, TAPS):
            filtered = filtered + window[tap][None, None, :] * piece[:, tap:tap + FR_DEV]
        filtered = filtered.astype(jnp.bfloat16).astype(jnp.float32)
        return jnp.einsum('kpj,nfj->kfpn', table, filtered)
    spectra = lax.map(channelize, jnp.arange(N_TM, dtype=jnp.int32))
    power = lax.optimization_barrier(jnp.sum(spectra * spectra, axis=(0, 2, 3))) / F
    scale = 1.0 / jnp.sqrt(power + 1e-06)
    equalized = (spectra * scale[None, :, None, None, :]).astype(jnp.bfloat16)

    def correlate(channel):
        block = equalized[:, channel].astype(jnp.float32)
        swapped = jnp.stack([block[:, :, 1], -block[:, :, 0]], axis=2)
        real_part = jnp.einsum('tfpa,tfpb->ab', block, block)
        imag_part = jnp.einsum('tfpa,tfpb->ab', swapped, block)
        return jnp.stack([real_part, imag_part], axis=0) / F
    return lax.map(correlate, jnp.arange(CH, dtype=jnp.int32))
```

```python
import functools
import itertools

import jax
import jax.numpy as jnp
import ml_dtypes
import numpy as np
from jax import lax
from jax.experimental import pallas as pl
from jax.experimental.pallas import tpu as pltpu
from jax.sharding import PartitionSpec as P

MESH = pl.DeviceIdType.MESH
FRAME = 1024
TAPS = 4
INPUTS = 64
FRAMES = 32
PAIRS = 16
CHIPS = 64
UNIT = 16
CHUNK = 16
ROWS = CHUNK * UNIT
PITCH = ROWS + 8
TOTAL = 512
LIFT = 2.0**32


def window_table():
    index = np.arange(TAPS * FRAME, dtype=np.float64)
    shifted = (index - TAPS * FRAME / 2 + 0.5) / FRAME
    shaped = np.sinc(shifted) * (0.54 - 0.46 * np.cos(2.0 * np.pi * index / (TAPS * FRAME - 1)))
    return (shaped.reshape(TAPS, FRAME) * LIFT).astype(np.float32)


def twiddle_table():
    chans = FRAME // 2
    turn = np.arange(chans)[:, None] * np.arange(FRAME)[None, :] % FRAME
    phase = turn.astype(np.float32) * np.float32(2.0 * np.pi / FRAME)
    phase = phase.astype(np.float64)
    pair = np.stack([np.cos(phase), -np.sin(phase)], axis=1)
    return pair.reshape(2 * chans, FRAME).astype(np.float32).astype(ml_dtypes.bfloat16)


def chip_order():
    offsets = list(itertools.product(range(4), repeat=3))[1:]
    orbits, seen = [], set()
    for start in offsets:
        if start in seen:
            continue
        orbit, now = [], start
        for _ in range(3):
            for one in (now, tuple((4 - v) % 4 for v in now)):
                if one not in orbit:
                    orbit.append(one)
            now = (now[1], now[2], now[0])
        seen.update(orbit)
        orbits.append(orbit)
    mixed = np.random.RandomState(1).permutation(len(orbits))
    return [o for i in mixed for o in orbits[i]] + [(0, 0, 0)]


ORDER = chip_order()


def channelize(volt, window, table, out, raw, filtered, rows, spectra, sendbuf, raw_sem, row_sem, send_sem, recv_sem, own_sem):
    row, column = lax.axis_index("inp"), lax.axis_index("tm")
    x, y, z, core = column // 4, row // 2, (row % 2) * 2 + (column // 2) % 2, column % 2
    me = row * 16 + column

    barrier = pltpu.get_barrier_semaphore()

    def greet(step, carry):
        other = lax.rem(me + step, 128)
        pl.semaphore_signal(barrier, inc=1, device_id=(other // 16, other % 16), device_id_type=MESH)
        return carry

    tiles = INPUTS // 16
    loads = [
        pltpu.make_async_copy(volt.at[pl.ds(16 * i, 16)], raw.at[pl.ds(16 * i, 16)], raw_sem.at[i])
        for i in range(tiles)
    ]
    for load in loads:
        load.start()
    lax.fori_loop(1, 128, greet, 0)

    places = []
    for k, (dx, dy, dz) in enumerate(ORDER):
        px, py, pz = lax.rem(x + dx, 4), lax.rem(y + dy, 4), lax.rem(z + dz, 4)
        inp, tm = py * 2 + pz // 2, px * 4 + lax.rem(pz, 2) * 2
        places.append((inp, tm))
        chip = inp * 8 + tm // 2
        source = table.at[pl.ds(pl.multiple_of(chip * UNIT, UNIT), UNIT)]
        pltpu.make_async_copy(source, rows.at[pl.ds(k * UNIT, UNIT)], row_sem.at[k // CHUNK]).start()

    for i in range(tiles):
        loads[i].wait()

        def filter_tile(j, carry, i=i):
            at = pl.multiple_of(j * 128, 128)
            taps = [window[pl.ds(k, 1), pl.ds(at, 128)] for k in range(TAPS)]
            held = []
            for f in range(FRAMES + TAPS - 1):
                held.append(raw[pl.ds(16 * i, 16), pl.ds(f * FRAME + at, 128)].astype(jnp.float32))
                if f >= TAPS - 1:
                    total = taps[0] * held[0]
                    for k in range(1, TAPS):
                        total = total + taps[k] * held[k]
                    held.pop(0)
                    g = f - TAPS + 1
                    filtered[pl.ds(g * INPUTS + 16 * i, 16), pl.ds(at, 128)] = total.astype(jnp.bfloat16)
            return carry

        lax.fori_loop(0, FRAME // 128, filter_tile, 0)

    copies = []
    for chunk in range(CHIPS // CHUNK):
        here = rows.at[pl.ds(chunk * ROWS, ROWS)]
        pltpu.make_async_copy(table.at[pl.ds(0, ROWS)], here, row_sem.at[chunk]).wait()

        def transform(n, carry, here=here):
            block = filtered[pl.ds(pl.multiple_of(n * 256, 256), 256), :]
            product = lax.dot_general(
                here[...], block, (((1,), (1,)), ((), ())), preferred_element_type=jnp.float32
            )
            for h in range(2):
                at = pl.multiple_of((2 * n + h) * PITCH, 8)
                spectra[pl.ds(at, ROWS), :] = product[:, h * 128 : (h + 1) * 128]
            return carry

        lax.fori_loop(0, PAIRS // 2, transform, 0)

        def gather(u, carry, chunk=chunk):
            for r in range(UNIT):
                part = spectra[pl.ds(u * UNIT + r, PAIRS, stride=PITCH), :]
                sendbuf[chunk * CHUNK + u, r] = part.astype(jnp.bfloat16)
            return carry

        lax.fori_loop(0, CHUNK, gather, 0)

        if chunk == 0:
            pl.semaphore_wait(barrier, 127)
        for k in range(chunk * CHUNK, (chunk + 1) * CHUNK):
            inp, tm = places[k]
            for turn in range(2):
                to = lax.rem(core + turn, 2)
                half = sendbuf.at[k, pl.ds(to * 8, 8)]
                if ORDER[k] == (0, 0, 0) and turn == 0:
                    copy = pltpu.make_async_copy(half, out.at[me], own_sem)
                else:
                    copy = pltpu.make_async_remote_copy(
                        src_ref=half,
                        dst_ref=out.at[me],
                        send_sem=send_sem.at[k, turn],
                        recv_sem=recv_sem.at[k, turn],
                        device_id=(inp, tm + to),
                        device_id_type=MESH,
                    )
                copy.start()
                copies.append(copy)
    for copy in copies:
        copy.wait()


def correlate(block, out, parts):
    lane = lax.broadcasted_iota(jnp.int32, (256, 128), 1)
    for p in range(2):
        for k in range(4):
            even = block[32 * k : 32 * k + 16, 0, p].reshape(256, 128)
            odd = block[32 * k + 16 : 32 * k + 32, 0, p].reshape(256, 128)
            first = jnp.concatenate([even[:, :64], odd[:, :64]], axis=1)
            second = jnp.concatenate([even[:, 64:], odd[:, 64:]], axis=1)
            parts[512 * p : 512 * p + 256, 128 * k : 128 * k + 128] = first
            parts[512 * p + 256 : 512 * p + 512, 128 * k : 128 * k + 128] = second
    dims = (((0,), (0,)), ((), ()))
    both = parts[...]
    real = lax.dot_general(both, both, dims, preferred_element_type=jnp.float32)
    cross = lax.dot_general(parts[512:, :], parts[:512, :], dims, preferred_element_type=jnp.float32)
    imag = cross - cross.T
    same = lax.broadcasted_iota(jnp.int32, (128, 128), 0) == lax.broadcasted_iota(jnp.int32, (128, 128), 1)
    along, down = [], []
    for k in range(4):
        tile = jnp.where(same, real[128 * k : 128 * k + 128, 128 * k : 128 * k + 128], 0.0)
        along.append(jnp.sum(tile, axis=0, keepdims=True))
        down.append(jnp.sum(tile, axis=1, keepdims=True))

    def scale(power):
        return lax.rsqrt(power * (LIFT**-2 / TOTAL) + 1e-06) * (1.0 / LIFT)

    along = scale(jnp.concatenate(along, axis=1)) * (1.0 / TOTAL)
    down = scale(jnp.concatenate(down, axis=0))
    out[0, 0] = real * along * down
    out[0, 1] = imag * along * down


def on_device(volt):
    block = pl.pallas_call(
        channelize,
        out_shape=jax.ShapeDtypeStruct((128, 8, PAIRS, 128), jnp.bfloat16),
        in_specs=[
            pl.BlockSpec(memory_space=pl.ANY),
            pl.BlockSpec(memory_space=pltpu.VMEM),
            pl.BlockSpec(memory_space=pl.ANY),
        ],
        out_specs=pl.BlockSpec(memory_space=pl.ANY),
        scratch_shapes=[
            pltpu.VMEM((INPUTS, (FRAMES + TAPS - 1) * FRAME), jnp.bfloat16),
            pltpu.VMEM((FRAMES * INPUTS, FRAME), jnp.bfloat16),
            pltpu.VMEM((CHIPS * UNIT, FRAME), jnp.bfloat16),
            pltpu.VMEM((PAIRS * PITCH, 128), jnp.float32),
            pltpu.VMEM((CHIPS, UNIT, PAIRS, 128), jnp.bfloat16),
            pltpu.SemaphoreType.DMA((INPUTS // 16,)),
            pltpu.SemaphoreType.DMA((CHIPS // CHUNK,)),
            pltpu.SemaphoreType.DMA((CHIPS, 2)),
            pltpu.SemaphoreType.DMA((CHIPS, 2)),
            pltpu.SemaphoreType.DMA,
        ],
        compiler_params=pltpu.CompilerParams(
            collective_id=0, has_side_effects=True, vmem_limit_bytes=48 << 20
        ),
        name="channelize",
    )(volt, jnp.asarray(window_table()), jnp.asarray(twiddle_table()))
    block = block.reshape(128, 4, 2, PAIRS, 128)
    return pl.pallas_call(
        correlate,
        grid=(4,),
        out_shape=jax.ShapeDtypeStruct((4, 2, 512, 512), jnp.float32),
        in_specs=[pl.BlockSpec((128, 1, 2, PAIRS, 128), lambda c: (0, c, 0, 0, 0))],
        out_specs=pl.BlockSpec((1, 2, 512, 512), lambda c: (c, 0, 0, 0)),
        scratch_shapes=[pltpu.VMEM((1024, 512), jnp.bfloat16)],
        compiler_params=pltpu.CompilerParams(vmem_limit_bytes=48 << 20),
        name="correlate",
    )(block)


def solution(mesh):
    return jax.shard_map(
        on_device,
        mesh=mesh,
        in_specs=(P("inp", "tm"),),
        out_specs=P(("inp", "tm"), None, None, None),
        check_vma=False,
    )
```

```python
import functools
import itertools

import jax
import jax.numpy as jnp
import ml_dtypes
import numpy as np
from jax import lax
from jax.experimental import pallas as pl
from jax.experimental.pallas import tpu as pltpu
from jax.sharding import PartitionSpec as P

MESH = pl.DeviceIdType.MESH
FRAME = 1024
TAPS = 4
INPUTS = 64
FRAMES = 32
HALF = 16
PAIRS = 8
CHIPS = 64
UNIT = 16
CHUNK = 16
ROWS = CHUNK * UNIT
PITCH = ROWS + 8
TOTAL = 512
LIFT = 2.0**32


def window_table():
    index = np.arange(TAPS * FRAME, dtype=np.float64)
    shifted = (index - TAPS * FRAME / 2 + 0.5) / FRAME
    shaped = np.sinc(shifted) * (0.54 - 0.46 * np.cos(2.0 * np.pi * index / (TAPS * FRAME - 1)))
    return (shaped.reshape(TAPS, FRAME) * LIFT).astype(np.float32)


def twiddle_table():
    chans = FRAME // 2
    turn = np.arange(chans)[:, None] * np.arange(FRAME)[None, :] % FRAME
    phase = turn.astype(np.float32) * np.float32(2.0 * np.pi / FRAME)
    phase = phase.astype(np.float64)
    pair = np.stack([np.cos(phase), -np.sin(phase)], axis=1)
    return pair.reshape(2 * chans, FRAME).astype(np.float32).astype(ml_dtypes.bfloat16)


def chip_order():
    offsets = list(itertools.product(range(4), repeat=3))[1:]
    orbits, seen = [], set()
    for start in offsets:
        if start in seen:
            continue
        orbit, now = [], start
        for _ in range(3):
            for one in (now, tuple((4 - v) % 4 for v in now)):
                if one not in orbit:
                    orbit.append(one)
            now = (now[1], now[2], now[0])
        seen.update(orbit)
        orbits.append(orbit)
    mixed = np.random.RandomState(1).permutation(len(orbits))
    return [o for i in mixed for o in orbits[i]] + [(0, 0, 0)]


ORDER = chip_order()


def channelize(volt, window, table, out, raw, filtered, taps, whole, rows, spectra, sendbuf, raw_sem, row_sem, send_sem, recv_sem, own_sem):
    row, column = lax.axis_index("inp"), lax.axis_index("tm")
    x, y, z, core = column // 4, row // 2, (row % 2) * 2 + (column // 2) % 2, column % 2
    me = row * 16 + column

    cuts = [(0, HALF + TAPS - 1), (HALF + TAPS - 1, FRAMES + TAPS - 1)]
    loads = []
    for h, (lo, hi) in enumerate(cuts):
        for i in range(INPUTS // 16):
            at = (pl.ds(16 * i, 16), pl.ds(lo * FRAME, (hi - lo) * FRAME))
            loads.append(pltpu.make_async_copy(volt.at[at], raw.at[at], raw_sem.at[h, i]))
    small = [
        pltpu.make_async_copy(window, taps, row_sem.at[0]),
        pltpu.make_async_copy(table, whole, row_sem.at[1]),
    ]
    for load in small[:1] + loads[:4] + small[1:] + loads[4:]:
        load.start()

    barrier = pltpu.get_barrier_semaphore()

    def greet(step, carry):
        other = lax.rem(me + step, 128)
        pl.semaphore_signal(barrier, inc=1, device_id=(other // 16, other % 16), device_id_type=MESH)
        return carry

    lax.fori_loop(1, 128, greet, 0)
    small[0].wait()

    copies = []
    for h in range(2):
        for i in range(INPUTS // 16):
            loads[4 * h + i].wait()

            def filter_tile(j, carry, i=i, h=h):
                at = pl.multiple_of(j * 128, 128)
                weight = [taps[pl.ds(k, 1), pl.ds(at, 128)] for k in range(TAPS)]
                held = []
                for f in range(HALF * h, HALF * h + HALF + TAPS - 1):
                    held.append(raw[pl.ds(16 * i, 16), pl.ds(f * FRAME + at, 128)].astype(jnp.float32))
                    if len(held) == TAPS:
                        total = weight[0] * held[0]
                        for k in range(1, TAPS):
                            total = total + weight[k] * held[k]
                        held.pop(0)
                        g = f - TAPS + 1
                        filtered[pl.ds(g * INPUTS + 16 * i, 16), pl.ds(at, 128)] = total.astype(jnp.bfloat16)
                return carry

            lax.fori_loop(0, FRAME // 128, filter_tile, 0)
        if h == 0:
            small[1].wait()

        for chunk in range(CHIPS // CHUNK):
            units = range(chunk * CHUNK, (chunk + 1) * CHUNK)
            places = []
            for k in units:
                dx, dy, dz = ORDER[k]
                px, py, pz = lax.rem(x + dx, 4), lax.rem(y + dy, 4), lax.rem(z + dz, 4)
                inp, tm = py * 2 + pz // 2, px * 4 + lax.rem(pz, 2) * 2
                places.append((inp, tm))
                if h == 0:
                    chip = inp * 8 + tm // 2
                    rows[k * UNIT : (k + 1) * UNIT, :] = whole[pl.ds(pl.multiple_of(chip * UNIT, UNIT), UNIT), :]
            product = lax.dot_general(
                rows[chunk * ROWS : (chunk + 1) * ROWS, :],
                filtered[h * HALF * INPUTS : (h + 1) * HALF * INPUTS, :],
                (((1,), (1,)), ((), ())),
                preferred_element_type=jnp.float32,
            )
            for n in range(PAIRS):
                spectra[n * PITCH : n * PITCH + ROWS, :] = product[:, n * 128 : (n + 1) * 128]

            def gather(u, carry, chunk=chunk, h=h):
                for r in range(UNIT // 2):
                    pair = [spectra[pl.ds(u * UNIT + 2 * r + p, PAIRS, stride=PITCH), :] for p in range(2)]
                    sendbuf[h, chunk * CHUNK + u, r] = jnp.concatenate(pair, axis=0).astype(jnp.bfloat16)
                return carry

            lax.fori_loop(0, CHUNK, gather, 0)

            if h == 0 and chunk == 0:
                pl.semaphore_wait(barrier, 127)
            for k in units:
                inp, tm = places[k - units.start]
                for turn in range(2):
                    to = lax.rem(core + turn, 2)
                    part = sendbuf.at[h, k, pl.ds(to * 4, 4)]
                    if ORDER[k] == (0, 0, 0) and turn == 0:
                        copy = pltpu.make_async_copy(part, out.at[h, me], own_sem.at[h])
                    else:
                        copy = pltpu.make_async_remote_copy(
                            src_ref=part,
                            dst_ref=out.at[h, me],
                            send_sem=send_sem.at[h, k, turn],
                            recv_sem=recv_sem.at[h, k, turn],
                            device_id=(inp, tm + to),
                            device_id_type=MESH,
                        )
                    copy.start()
                    copies.append(copy)
    for copy in copies:
        copy.wait()


def correlate(block, out, held, turned, made, in_sem, out_sem):
    loads = [pltpu.make_async_copy(block.at[:, :, c], held.at[c], in_sem.at[c]) for c in range(4)]
    for load in loads:
        load.start()
    nt = (((1,), (1,)), ((), ()))
    same = lax.broadcasted_iota(jnp.int32, (128, 128), 0) == lax.broadcasted_iota(jnp.int32, (128, 128), 1)

    def scale(power):
        return lax.rsqrt(power * (LIFT**-2 / TOTAL) + 1e-06) * (1.0 / LIFT)

    stores = []
    for c in range(4):
        s = c % 2
        loads[c].wait()
        for p in range(2):
            for h in range(2):
                for k in range(4):
                    even = held[c, h, 32 * k : 32 * k + 16, 8 * p : 8 * p + 8, :].reshape(128, 128)
                    odd = held[c, h, 32 * k + 16 : 32 * k + 32, 8 * p : 8 * p + 8, :].reshape(128, 128)
                    for f in range(2):
                        cut = slice(64 * f, 64 * f + 64)
                        tile = jnp.concatenate([even[:, cut], odd[:, cut]], axis=1)
                        at = 512 * p + 256 * h + 128 * f
                        turned[s, 128 * k : 128 * k + 128, at : at + 128] = tile.T

        def dot(a, b, s=s):
            left, right = [
                turned[s, 256 * i : 256 * i + 256, :]
                if p is None
                else turned[s, 256 * i : 256 * i + 256, 512 * p : 512 * p + 512]
                for i, p in (a, b)
            ]
            return lax.dot_general(left, right, nt, preferred_element_type=jnp.float32)

        if c >= 2:
            for store in stores[2 * c - 4 : 2 * c - 2]:
                store.wait()
        own = [dot((i, None), (i, None)) for i in range(2)]
        along, down = [], []
        for block_sum in own:
            tiles = [
                jnp.where(same, block_sum[128 * k : 128 * k + 128, 128 * k : 128 * k + 128], 0.0) for k in range(2)
            ]
            along.append(
                scale(jnp.concatenate([jnp.sum(t, axis=0, keepdims=True) for t in tiles], axis=1)) * (1.0 / TOTAL)
            )
            down.append(scale(jnp.concatenate([jnp.sum(t, axis=1, keepdims=True) for t in tiles], axis=0)))
        for i in range(2):
            cut = slice(256 * i, 256 * i + 256)
            made[s, 0, cut, cut] = own[i] * along[i] * down[i]
        mixed = dot((0, None), (1, None)) * along[1] * down[0]
        made[s, 0, 0:256, 256:512] = mixed
        made[s, 0, 256:512, 0:256] = mixed.T
        stores.append(pltpu.make_async_copy(made.at[s, 0], out.at[c, 0], out_sem.at[s, 0]))
        stores[-1].start()
        for i in range(2):
            cut = slice(256 * i, 256 * i + 256)
            cross = dot((i, 1), (i, 0))
            made[s, 1, cut, cut] = (cross - cross.T) * along[i] * down[i]
        mixed = (dot((0, 1), (1, 0)) - dot((0, 0), (1, 1))) * along[1] * down[0]
        made[s, 1, 0:256, 256:512] = mixed
        made[s, 1, 256:512, 0:256] = -mixed.T
        stores.append(pltpu.make_async_copy(made.at[s, 1], out.at[c, 1], out_sem.at[s, 1]))
        stores[-1].start()
    for store in stores[4:]:
        store.wait()


def on_device(volt):
    whole = pl.BlockSpec(memory_space=pl.ANY)
    block = pl.pallas_call(
        channelize,
        out_shape=jax.ShapeDtypeStruct((2, 128, 4, 16, 128), jnp.bfloat16),
        in_specs=[whole, whole, whole],
        out_specs=whole,
        scratch_shapes=[
            pltpu.VMEM((INPUTS, (FRAMES + TAPS - 1) * FRAME), jnp.bfloat16),
            pltpu.VMEM((FRAMES * INPUTS, FRAME), jnp.bfloat16),
            pltpu.VMEM((TAPS, FRAME), jnp.float32),
            pltpu.VMEM((CHIPS * UNIT, FRAME), jnp.bfloat16),
            pltpu.VMEM((CHIPS * UNIT, FRAME), jnp.bfloat16),
            pltpu.VMEM((PAIRS * PITCH, 128), jnp.float32),
            pltpu.VMEM((2, CHIPS, 8, 16, 128), jnp.bfloat16),
            pltpu.SemaphoreType.DMA((2, INPUTS // 16)),
            pltpu.SemaphoreType.DMA((2,)),
            pltpu.SemaphoreType.DMA((2, CHIPS, 2)),
            pltpu.SemaphoreType.DMA((2, CHIPS, 2)),
            pltpu.SemaphoreType.DMA((2,)),
        ],
        compiler_params=pltpu.CompilerParams(
            collective_id=0, has_side_effects=True, vmem_limit_bytes=60 << 20
        ),
        name="channelize",
    )(volt, jnp.asarray(window_table()), jnp.asarray(twiddle_table()))
    return pl.pallas_call(
        correlate,
        out_shape=jax.ShapeDtypeStruct((4, 2, 512, 512), jnp.float32),
        in_specs=[whole],
        out_specs=whole,
        scratch_shapes=[
            pltpu.VMEM((4, 2, 128, 16, 128), jnp.bfloat16),
            pltpu.VMEM((2, 512, 1024), jnp.bfloat16),
            pltpu.VMEM((2, 2, 512, 512), jnp.float32),
            pltpu.SemaphoreType.DMA((4,)),
            pltpu.SemaphoreType.DMA((2, 2)),
        ],
        compiler_params=pltpu.CompilerParams(vmem_limit_bytes=60 << 20),
        name="correlate",
    )(block)


def solution(mesh):
    return jax.shard_map(
        on_device,
        mesh=mesh,
        in_specs=(P("inp", "tm"),),
        out_specs=P(("inp", "tm"), None, None, None),
        check_vma=False,
    )
```

```python
import functools
import itertools

import jax
import jax.numpy as jnp
import ml_dtypes
import numpy as np
from jax import lax
from jax.experimental import pallas as pl
from jax.experimental.pallas import tpu as pltpu
from jax.sharding import PartitionSpec as P

MESH = pl.DeviceIdType.MESH
FRAME = 1024
TAPS = 4
INPUTS = 64
FRAMES = 32
HALF = 16
PAIRS = 8
CHIPS = 64
UNIT = 16
CHUNK = 16
ROWS = CHUNK * UNIT
PITCH = ROWS + 8
TOTAL = 512
LIFT = 2.0**32


def window_table():
    index = np.arange(TAPS * FRAME, dtype=np.float64)
    shifted = (index - TAPS * FRAME / 2 + 0.5) / FRAME
    shaped = np.sinc(shifted) * (0.54 - 0.46 * np.cos(2.0 * np.pi * index / (TAPS * FRAME - 1)))
    return (shaped.reshape(TAPS, FRAME) * LIFT).astype(np.float32)


def twiddle_table():
    chans = FRAME // 2
    turn = np.arange(chans)[:, None] * np.arange(FRAME)[None, :] % FRAME
    phase = turn.astype(np.float32) * np.float32(2.0 * np.pi / FRAME)
    phase = phase.astype(np.float64)
    pair = np.stack([np.cos(phase), -np.sin(phase)], axis=1)
    return pair.reshape(2 * chans, FRAME).astype(np.float32).astype(ml_dtypes.bfloat16)


def chip_order():
    offsets = list(itertools.product(range(4), repeat=3))[1:]
    orbits, seen = [], set()
    for start in offsets:
        if start in seen:
            continue
        orbit, now = [], start
        for _ in range(3):
            for one in (now, tuple((4 - v) % 4 for v in now)):
                if one not in orbit:
                    orbit.append(one)
            now = (now[1], now[2], now[0])
        seen.update(orbit)
        orbits.append(orbit)
    mixed = np.random.RandomState(1).permutation(len(orbits))
    return [o for i in mixed for o in orbits[i]] + [(0, 0, 0)]


ORDER = chip_order()


def channelize(volt, window, table, out, raw, filtered, taps, whole, rows, spectra, sendbuf, raw_sem, row_sem, send_sem, recv_sem, own_sem):
    row, column = lax.axis_index("inp"), lax.axis_index("tm")
    x, y, z, core = column // 4, row // 2, (row % 2) * 2 + (column // 2) % 2, column % 2
    me = row * 16 + column

    cuts = [(0, HALF + TAPS - 1), (HALF + TAPS - 1, FRAMES + TAPS - 1)]
    loads = []
    for h, (lo, hi) in enumerate(cuts):
        for i in range(INPUTS // 16):
            at = (pl.ds(16 * i, 16), pl.ds(lo * FRAME, (hi - lo) * FRAME))
            loads.append(pltpu.make_async_copy(volt.at[at], raw.at[at], raw_sem.at[h, i]))
    small = [
        pltpu.make_async_copy(window, taps, row_sem.at[0]),
        pltpu.make_async_copy(table, whole, row_sem.at[1]),
    ]
    for load in small[:1] + loads[:4] + small[1:] + loads[4:]:
        load.start()

    def onward(at, step):
        there = at + step
        return jnp.where(there >= 4, there - 4, there)

    xs = [onward(x, d) * 4 for d in range(4)]
    ys = [onward(y, d) * 2 for d in range(4)]
    upper = [jnp.where(onward(z, d) >= 2, 1, 0) for d in range(4)]
    lower = [(onward(z, d) - 2 * upper[d]) * 2 for d in range(4)]
    cores = [core, 1 - core]

    def chip_at(offset):
        dx, dy, dz = offset
        return ys[dy] + upper[dz], xs[dx] + lower[dz]

    barrier = pltpu.get_barrier_semaphore()
    for offset in ORDER:
        inp, tm = chip_at(offset)
        for turn in range(2):
            if (offset, turn) != ((0, 0, 0), 0):
                pl.semaphore_signal(barrier, inc=1, device_id=(inp, tm + cores[turn]), device_id_type=MESH)
    small[0].wait()

    own = []
    for h in range(2):
        for i in range(INPUTS // 16):
            loads[4 * h + i].wait()

            def filter_tile(j, carry, i=i, h=h):
                at = pl.multiple_of(j * 128, 128)
                weight = [taps[pl.ds(k, 1), pl.ds(at, 128)] for k in range(TAPS)]
                held = []
                for f in range(HALF * h, HALF * h + HALF + TAPS - 1):
                    held.append(raw[pl.ds(16 * i, 16), pl.ds(f * FRAME + at, 128)].astype(jnp.float32))
                    if len(held) == TAPS:
                        total = weight[0] * held[0]
                        for k in range(1, TAPS):
                            total = total + weight[k] * held[k]
                        held.pop(0)
                        g = f - TAPS + 1
                        filtered[pl.ds(g * INPUTS + 16 * i, 16), pl.ds(at, 128)] = total.astype(jnp.bfloat16)
                return carry

            lax.fori_loop(0, FRAME // 128, filter_tile, 0)
        if h == 0:
            small[1].wait()

        for chunk in range(CHIPS // CHUNK):
            units = range(chunk * CHUNK, (chunk + 1) * CHUNK)
            if h == 0:
                for k in units:
                    inp, tm = chip_at(ORDER[k])
                    at = pl.multiple_of(inp * (8 * UNIT) + tm * (UNIT // 2), UNIT)
                    rows[k * UNIT : (k + 1) * UNIT, :] = whole[pl.ds(at, UNIT), :]
            product = lax.dot_general(
                rows[chunk * ROWS : (chunk + 1) * ROWS, :],
                filtered[h * HALF * INPUTS : (h + 1) * HALF * INPUTS, :],
                (((1,), (1,)), ((), ())),
                preferred_element_type=jnp.float32,
            )
            for n in range(PAIRS):
                spectra[n * PITCH : n * PITCH + ROWS, :] = product[:, n * 128 : (n + 1) * 128]

            def gather(u, carry, chunk=chunk, h=h):
                for r in range(UNIT // 2):
                    pair = [spectra[pl.ds(u * UNIT + 2 * r + p, PAIRS, stride=PITCH), :] for p in range(2)]
                    sendbuf[h, 2 * (chunk * CHUNK + u) + r // 4, r % 4] = jnp.concatenate(pair, axis=0).astype(jnp.bfloat16)
                return carry

            lax.fori_loop(0, CHUNK, gather, 0)

            if h == 0 and chunk == 0:
                pl.semaphore_wait(barrier, 127)
            for k in units:
                inp, tm = chip_at(ORDER[k])
                for turn in range(2):
                    to = cores[turn]
                    part = sendbuf.at[h, 2 * k + to]
                    if ORDER[k] == (0, 0, 0) and turn == 0:
                        copy = pltpu.make_async_copy(part, out.at[h, me], own_sem.at[h])
                        own.append(copy)
                    else:
                        copy = pltpu.make_async_remote_copy(
                            src_ref=part,
                            dst_ref=out.at[h, me],
                            send_sem=send_sem.at[h],
                            recv_sem=recv_sem.at[h],
                            device_id=(inp, tm + to),
                            device_id_type=MESH,
                        )
                    copy.start()
    for h in range(2):
        own[h].wait()
        every = pltpu.make_async_remote_copy(
            src_ref=sendbuf.at[h, pl.ds(0, 127)],
            dst_ref=out.at[h, pl.ds(0, 127)],
            send_sem=send_sem.at[h],
            recv_sem=recv_sem.at[h],
            device_id=(row, column - core + cores[1]),
            device_id_type=MESH,
        )
        every.wait()


def correlate(block, out, held, turned, made, in_sem, out_sem):
    loads = [pltpu.make_async_copy(block.at[:, :, c], held.at[c], in_sem.at[c]) for c in range(4)]
    for load in loads:
        load.start()
    nt = (((1,), (1,)), ((), ()))
    same = lax.broadcasted_iota(jnp.int32, (128, 128), 0) == lax.broadcasted_iota(jnp.int32, (128, 128), 1)

    def scale(power):
        return lax.rsqrt(power * (LIFT**-2 / TOTAL) + 1e-06) * (1.0 / LIFT)

    stores = []
    for c in range(4):
        s = c % 2
        loads[c].wait()
        for p in range(2):
            for h in range(2):
                for i in range(8):
                    tile = held[c, h, 16 * i : 16 * i + 16, 8 * p : 8 * p + 8, :].reshape(128, 128).T
                    for f in range(2):
                        at = 512 * p + 256 * h + 128 * f
                        turned[s, 64 * i : 64 * i + 64, at : at + 128] = tile[64 * f : 64 * f + 64, :]

        def dot(a, b, s=s):
            left, right = [
                turned[s, 256 * i : 256 * i + 256, :]
                if p is None
                else turned[s, 256 * i : 256 * i + 256, 512 * p : 512 * p + 512]
                for i, p in (a, b)
            ]
            return lax.dot_general(left, right, nt, preferred_element_type=jnp.float32)

        if c >= 2:
            for store in stores[2 * c - 4 : 2 * c - 2]:
                store.wait()
        own = [dot((i, None), (i, None)) for i in range(2)]
        along, down = [], []
        for block_sum in own:
            tiles = [
                jnp.where(same, block_sum[128 * k : 128 * k + 128, 128 * k : 128 * k + 128], 0.0) for k in range(2)
            ]
            along.append(
                scale(jnp.concatenate([jnp.sum(t, axis=0, keepdims=True) for t in tiles], axis=1)) * (1.0 / TOTAL)
            )
            down.append(scale(jnp.concatenate([jnp.sum(t, axis=1, keepdims=True) for t in tiles], axis=0)))
        for i in range(2):
            cut = slice(256 * i, 256 * i + 256)
            made[s, 0, cut, cut] = own[i] * along[i] * down[i]
        mixed = dot((0, None), (1, None)) * along[1] * down[0]
        made[s, 0, 0:256, 256:512] = mixed
        made[s, 0, 256:512, 0:256] = mixed.T
        stores.append(pltpu.make_async_copy(made.at[s, 0], out.at[c, 0], out_sem.at[s, 0]))
        stores[-1].start()
        for i in range(2):
            cut = slice(256 * i, 256 * i + 256)
            cross = dot((i, 1), (i, 0))
            made[s, 1, cut, cut] = (cross - cross.T) * along[i] * down[i]
        mixed = (dot((0, 1), (1, 0)) - dot((0, 0), (1, 1))) * along[1] * down[0]
        made[s, 1, 0:256, 256:512] = mixed
        made[s, 1, 256:512, 0:256] = -mixed.T
        stores.append(pltpu.make_async_copy(made.at[s, 1], out.at[c, 1], out_sem.at[s, 1]))
        stores[-1].start()
    for store in stores[4:]:
        store.wait()


def on_device(volt):
    whole = pl.BlockSpec(memory_space=pl.ANY)
    block = pl.pallas_call(
        channelize,
        out_shape=jax.ShapeDtypeStruct((2, 128, 4, 16, 128), jnp.bfloat16),
        in_specs=[whole, whole, whole],
        out_specs=whole,
        scratch_shapes=[
            pltpu.VMEM((INPUTS, (FRAMES + TAPS - 1) * FRAME), jnp.bfloat16),
            pltpu.VMEM((FRAMES * INPUTS, FRAME), jnp.bfloat16),
            pltpu.VMEM((TAPS, FRAME), jnp.float32),
            pltpu.VMEM((CHIPS * UNIT, FRAME), jnp.bfloat16),
            pltpu.VMEM((CHIPS * UNIT, FRAME), jnp.bfloat16),
            pltpu.VMEM((PAIRS * PITCH, 128), jnp.float32),
            pltpu.VMEM((2, 2 * CHIPS, 4, 16, 128), jnp.bfloat16),
            pltpu.SemaphoreType.DMA((2, INPUTS // 16)),
            pltpu.SemaphoreType.DMA((2,)),
            pltpu.SemaphoreType.DMA((2,)),
            pltpu.SemaphoreType.DMA((2,)),
            pltpu.SemaphoreType.DMA((2,)),
        ],
        compiler_params=pltpu.CompilerParams(
            collective_id=0, has_side_effects=True, vmem_limit_bytes=60 << 20
        ),
        name="channelize",
    )(volt, jnp.asarray(window_table()), jnp.asarray(twiddle_table()))
    return pl.pallas_call(
        correlate,
        out_shape=jax.ShapeDtypeStruct((4, 2, 512, 512), jnp.float32),
        in_specs=[whole],
        out_specs=whole,
        scratch_shapes=[
            pltpu.VMEM((4, 2, 128, 16, 128), jnp.bfloat16),
            pltpu.VMEM((2, 512, 1024), jnp.bfloat16),
            pltpu.VMEM((2, 2, 512, 512), jnp.float32),
            pltpu.SemaphoreType.DMA((4,)),
            pltpu.SemaphoreType.DMA((2, 2)),
        ],
        compiler_params=pltpu.CompilerParams(vmem_limit_bytes=60 << 20),
        name="correlate",
    )(block)


def solution(mesh):
    return jax.shard_map(
        on_device,
        mesh=mesh,
        in_specs=(P("inp", "tm"),),
        out_specs=P(("inp", "tm"), None, None, None),
        check_vma=False,
    )
```

```python
import functools
import itertools

import jax
import jax.numpy as jnp
import ml_dtypes
import numpy as np
from jax import lax
from jax.experimental import pallas as pl
from jax.experimental.pallas import tpu as pltpu
from jax.sharding import PartitionSpec as P

MESH = pl.DeviceIdType.MESH
FRAME = 1024
TAPS = 4
INPUTS = 64
FRAMES = 32
HALF = 16
PAIRS = 8
CHIPS = 64
UNIT = 16
CHUNK = 16
ROWS = CHUNK * UNIT
PITCH = ROWS + 8
TOTAL = 512
LIFT = 2.0**32


def window_table():
    index = np.arange(TAPS * FRAME, dtype=np.float64)
    shifted = (index - TAPS * FRAME / 2 + 0.5) / FRAME
    shaped = np.sinc(shifted) * (0.54 - 0.46 * np.cos(2.0 * np.pi * index / (TAPS * FRAME - 1)))
    return (shaped.reshape(TAPS, FRAME) * LIFT).astype(np.float32)


def twiddle_table():
    chans = FRAME // 2
    turn = np.arange(chans)[:, None] * np.arange(FRAME)[None, :] % FRAME
    phase = turn.astype(np.float32) * np.float32(2.0 * np.pi / FRAME)
    phase = phase.astype(np.float64)
    pair = np.stack([np.cos(phase), -np.sin(phase)], axis=1)
    return pair.reshape(2 * chans, FRAME).astype(np.float32).astype(ml_dtypes.bfloat16)


def chip_orders():
    offsets = list(itertools.product(range(4), repeat=3))[1:]
    orbits, seen = [], set()
    for start in offsets:
        if start in seen:
            continue
        orbit, now = [], start
        for _ in range(3):
            for one in (now, tuple((4 - v) % 4 for v in now)):
                if one not in orbit:
                    orbit.append(one)
            now = (now[1], now[2], now[0])
        seen.update(orbit)
        orbits.append(orbit)
    mixed = [orbits[i] for i in np.random.RandomState(1).permutation(len(orbits))]
    falling = sorted(orbits, key=lambda orbit: -sum(min(v, 4 - v) for v in orbit[0]))
    return [[o for orbit in order for o in orbit] + [(0, 0, 0)] for order in (mixed, falling)]


ORDERS = chip_orders()


def channelize(volt, window, table, out, raw, filtered, taps, whole, rows, spectra, sendbuf, raw_sem, row_sem, send_sem, recv_sem, own_sem):
    row, column = lax.axis_index("inp"), lax.axis_index("tm")
    x, y, z, core = column // 4, row // 2, (row % 2) * 2 + (column // 2) % 2, column % 2
    me = row * 16 + column

    cuts = [(0, HALF + TAPS - 1), (HALF + TAPS - 1, FRAMES + TAPS - 1)]
    loads = []
    for h, (lo, hi) in enumerate(cuts):
        for i in range(INPUTS // 16):
            at = (pl.ds(16 * i, 16), pl.ds(lo * FRAME, (hi - lo) * FRAME))
            loads.append(pltpu.make_async_copy(volt.at[at], raw.at[at], raw_sem.at[h, i]))
    small = [
        pltpu.make_async_copy(window, taps, row_sem.at[0]),
        pltpu.make_async_copy(table, whole, row_sem.at[1]),
    ]
    for load in small[:1] + loads[:4] + small[1:] + loads[4:]:
        load.start()

    def onward(at, step):
        there = at + step
        return jnp.where(there >= 4, there - 4, there)

    xs = [onward(x, d) * 4 for d in range(4)]
    ys = [onward(y, d) * 2 for d in range(4)]
    upper = [jnp.where(onward(z, d) >= 2, 1, 0) for d in range(4)]
    lower = [(onward(z, d) - 2 * upper[d]) * 2 for d in range(4)]
    cores = [core, 1 - core]

    def chip_at(offset):
        dx, dy, dz = offset
        return ys[dy] + upper[dz], xs[dx] + lower[dz]

    barrier = pltpu.get_barrier_semaphore()
    for offset in ORDERS[0]:
        inp, tm = chip_at(offset)
        for turn in range(2):
            if (offset, turn) != ((0, 0, 0), 0):
                pl.semaphore_signal(barrier, inc=1, device_id=(inp, tm + cores[turn]), device_id_type=MESH)
    small[0].wait()

    own = []
    for h in range(2):
        for i in range(INPUTS // 16):
            loads[4 * h + i].wait()

            def filter_tile(j, carry, i=i, h=h):
                at = pl.multiple_of(j * 128, 128)
                weight = [taps[pl.ds(k, 1), pl.ds(at, 128)] for k in range(TAPS)]
                held = []
                for f in range(HALF * h, HALF * h + HALF + TAPS - 1):
                    held.append(raw[pl.ds(16 * i, 16), pl.ds(f * FRAME + at, 128)].astype(jnp.float32))
                    if len(held) == TAPS:
                        total = weight[0] * held[0]
                        for k in range(1, TAPS):
                            total = total + weight[k] * held[k]
                        held.pop(0)
                        g = f - TAPS + 1
                        filtered[pl.ds(g * INPUTS + 16 * i, 16), pl.ds(at, 128)] = total.astype(jnp.bfloat16)
                return carry

            lax.fori_loop(0, FRAME // 128, filter_tile, 0)
        if h == 0:
            small[1].wait()

        for chunk in range(CHIPS // CHUNK):
            units = range(chunk * CHUNK, (chunk + 1) * CHUNK)
            for k in units:
                inp, tm = chip_at(ORDERS[h][k])
                at = pl.multiple_of(inp * (8 * UNIT) + tm * (UNIT // 2), UNIT)
                rows[k * UNIT : (k + 1) * UNIT, :] = whole[pl.ds(at, UNIT), :]
            product = lax.dot_general(
                rows[chunk * ROWS : (chunk + 1) * ROWS, :],
                filtered[h * HALF * INPUTS : (h + 1) * HALF * INPUTS, :],
                (((1,), (1,)), ((), ())),
                preferred_element_type=jnp.float32,
            )
            for n in range(PAIRS):
                spectra[n * PITCH : n * PITCH + ROWS, :] = product[:, n * 128 : (n + 1) * 128]

            def gather(u, carry, chunk=chunk, h=h):
                for r in range(UNIT // 2):
                    pair = [spectra[pl.ds(u * UNIT + 2 * r + p, PAIRS, stride=PITCH), :] for p in range(2)]
                    sendbuf[h, 2 * (chunk * CHUNK + u) + r // 4, r % 4] = jnp.concatenate(pair, axis=0).astype(jnp.bfloat16)
                return carry

            lax.fori_loop(0, CHUNK, gather, 0)

            if h == 0 and chunk == 0:
                pl.semaphore_wait(barrier, 127)
            for k in units:
                inp, tm = chip_at(ORDERS[h][k])
                for turn in range(2):
                    to = cores[turn]
                    part = sendbuf.at[h, 2 * k + to]
                    if ORDERS[h][k] == (0, 0, 0) and turn == 0:
                        copy = pltpu.make_async_copy(part, out.at[h, me], own_sem.at[h])
                        own.append(copy)
                    else:
                        copy = pltpu.make_async_remote_copy(
                            src_ref=part,
                            dst_ref=out.at[h, me],
                            send_sem=send_sem.at[h],
                            recv_sem=recv_sem.at[h],
                            device_id=(inp, tm + to),
                            device_id_type=MESH,
                        )
                    copy.start()
    for h in range(2):
        own[h].wait()
        every = pltpu.make_async_remote_copy(
            src_ref=sendbuf.at[h, pl.ds(0, 127)],
            dst_ref=out.at[h, pl.ds(0, 127)],
            send_sem=send_sem.at[h],
            recv_sem=recv_sem.at[h],
            device_id=(row, column - core + cores[1]),
            device_id_type=MESH,
        )
        every.wait()


def correlate(block, out, held, turned, made, in_sem, out_sem):
    loads = [
        [pltpu.make_async_copy(block.at[h, :, c], held.at[c, h], in_sem.at[c, h]) for h in range(2)] for c in range(4)
    ]
    nt = (((1,), (1,)), ((), ()))
    same = lax.broadcasted_iota(jnp.int32, (128, 128), 0) == lax.broadcasted_iota(jnp.int32, (128, 128), 1)

    def scale(power):
        return lax.rsqrt(power * (LIFT**-2 / TOTAL) + 1e-06) * (1.0 / LIFT)

    def turn(c, h):
        for p in range(2):
            for i in range(8):
                tile = held[c, h, 16 * i : 16 * i + 16, 8 * p : 8 * p + 8, :].reshape(128, 128).T
                for f in range(2):
                    at = 512 * p + 256 * h + 128 * f
                    turned[c % 2, 64 * i : 64 * i + 64, at : at + 128] = tile[64 * f : 64 * f + 64, :]

    def store(c, p, rows, first):
        stores.append(
            pltpu.make_async_copy(
                made.at[c, p, pl.ds(first, rows)], out.at[c, p, pl.ds(first, rows)], out_sem.at[c, p, first // 256]
            )
        )
        stores[-1].start()

    stores = []
    for c in range(4):
        for h in range(2):
            loads[c][h].start()
    for h in range(2):
        loads[0][h].wait()
        turn(0, h)
    for c in range(4):
        s = c % 2

        def dot(a, b, s=s):
            left, right = [
                turned[s, 256 * i : 256 * i + 256, :]
                if p is None
                else turned[s, 256 * i : 256 * i + 256, 512 * p : 512 * p + 512]
                for i, p in (a, b)
            ]
            return lax.dot_general(left, right, nt, preferred_element_type=jnp.float32)

        if c + 1 < 4:
            for h in range(2):
                loads[c + 1][h].wait()
            for h in range(2):
                turn(c + 1, h)
        along, down = [], []
        for i in range(2):
            cut = slice(256 * i, 256 * i + 256)
            total = dot((i, None), (i, None))
            tiles = [jnp.where(same, total[128 * k : 128 * k + 128, 128 * k : 128 * k + 128], 0.0) for k in range(2)]
            along.append(
                scale(jnp.concatenate([jnp.sum(t, axis=0, keepdims=True) for t in tiles], axis=1)) * (1.0 / TOTAL)
            )
            down.append(scale(jnp.concatenate([jnp.sum(t, axis=1, keepdims=True) for t in tiles], axis=0)))
            made[c, 0, cut, cut] = total * along[i] * down[i]
        mixed = dot((0, None), (1, None)) * along[1] * down[0]
        made[c, 0, 0:256, 256:512] = mixed
        made[c, 0, 256:512, 0:256] = mixed.T
        store(c, 0, 512, 0)
        mixed = (dot((0, 1), (1, 0)) - dot((0, 0), (1, 1))) * along[1] * down[0]
        made[c, 1, 0:256, 256:512] = mixed
        made[c, 1, 256:512, 0:256] = -mixed.T
        for i in range(2):
            cut = slice(256 * i, 256 * i + 256)
            cross = dot((i, 1), (i, 0))
            made[c, 1, cut, cut] = (cross - cross.T) * along[i] * down[i]
            store(c, 1, 256, 256 * i)
    for one in stores:
        one.wait()


def on_device(volt):
    whole = pl.BlockSpec(memory_space=pl.ANY)
    block = pl.pallas_call(
        channelize,
        out_shape=jax.ShapeDtypeStruct((2, 128, 4, 16, 128), jnp.bfloat16),
        in_specs=[whole, whole, whole],
        out_specs=whole,
        scratch_shapes=[
            pltpu.VMEM((INPUTS, (FRAMES + TAPS - 1) * FRAME), jnp.bfloat16),
            pltpu.VMEM((FRAMES * INPUTS, FRAME), jnp.bfloat16),
            pltpu.VMEM((TAPS, FRAME), jnp.float32),
            pltpu.VMEM((CHIPS * UNIT, FRAME), jnp.bfloat16),
            pltpu.VMEM((CHIPS * UNIT, FRAME), jnp.bfloat16),
            pltpu.VMEM((PAIRS * PITCH, 128), jnp.float32),
            pltpu.VMEM((2, 2 * CHIPS, 4, 16, 128), jnp.bfloat16),
            pltpu.SemaphoreType.DMA((2, INPUTS // 16)),
            pltpu.SemaphoreType.DMA((2,)),
            pltpu.SemaphoreType.DMA((2,)),
            pltpu.SemaphoreType.DMA((2,)),
            pltpu.SemaphoreType.DMA((2,)),
        ],
        compiler_params=pltpu.CompilerParams(
            collective_id=0, has_side_effects=True, vmem_limit_bytes=60 << 20
        ),
        name="channelize",
    )(volt, jnp.asarray(window_table()), jnp.asarray(twiddle_table()))
    return pl.pallas_call(
        correlate,
        out_shape=jax.ShapeDtypeStruct((4, 2, 512, 512), jnp.float32),
        in_specs=[whole],
        out_specs=whole,
        scratch_shapes=[
            pltpu.VMEM((4, 2, 128, 16, 128), jnp.bfloat16),
            pltpu.VMEM((2, 512, 1024), jnp.bfloat16),
            pltpu.VMEM((4, 2, 512, 512), jnp.float32),
            pltpu.SemaphoreType.DMA((4, 2)),
            pltpu.SemaphoreType.DMA((4, 2, 2)),
        ],
        compiler_params=pltpu.CompilerParams(vmem_limit_bytes=60 << 20),
        name="correlate",
    )(block)


def solution(mesh):
    return jax.shard_map(
        on_device,
        mesh=mesh,
        in_specs=(P("inp", "tm"),),
        out_specs=P(("inp", "tm"), None, None, None),
        check_vma=False,
    )
```

```python
import functools
import itertools

import jax
import jax.numpy as jnp
import ml_dtypes
import numpy as np
from jax import lax
from jax.experimental import pallas as pl
from jax.experimental.pallas import tpu as pltpu
from jax.sharding import PartitionSpec as P

MESH = pl.DeviceIdType.MESH
FRAME = 1024
TAPS = 4
INPUTS = 64
FRAMES = 32
HALF = 16
PAIRS = 8
CHIPS = 64
UNIT = 16
CHUNK = 16
ROWS = CHUNK * UNIT
PITCH = ROWS + 8
TOTAL = 512
LIFT = 2.0**32


def window_table():
    index = np.arange(TAPS * FRAME, dtype=np.float64)
    shifted = (index - TAPS * FRAME / 2 + 0.5) / FRAME
    shaped = np.sinc(shifted) * (0.54 - 0.46 * np.cos(2.0 * np.pi * index / (TAPS * FRAME - 1)))
    return (shaped.reshape(TAPS, FRAME) * LIFT).astype(np.float32)


def twiddle_table():
    chans = FRAME // 2
    turn = np.arange(chans)[:, None] * np.arange(FRAME)[None, :] % FRAME
    phase = turn.astype(np.float32) * np.float32(2.0 * np.pi / FRAME)
    phase = phase.astype(np.float64)
    pair = np.stack([np.cos(phase), -np.sin(phase)], axis=1)
    return pair.reshape(2 * chans, FRAME).astype(np.float32).astype(ml_dtypes.bfloat16)


def chip_orders():
    offsets = list(itertools.product(range(4), repeat=3))[1:]
    orbits, seen = [], set()
    for start in offsets:
        if start in seen:
            continue
        orbit, now = [], start
        for _ in range(3):
            for one in (now, tuple((4 - v) % 4 for v in now)):
                if one not in orbit:
                    orbit.append(one)
            now = (now[1], now[2], now[0])
        seen.update(orbit)
        orbits.append(orbit)
    mixed = [orbits[i] for i in np.random.RandomState(1).permutation(len(orbits))]
    falling = sorted(orbits, key=lambda orbit: -sum(min(v, 4 - v) for v in orbit[0]))
    return [[o for orbit in order for o in orbit] + [(0, 0, 0)] for order in (mixed, falling)]


ORDERS = chip_orders()


ROUNDS = [(0, 1, 0, 2), (1, 1, 0, 2), (0, 2, 2, 2)]


def turn(held, turned, h):
    for p in range(2):
        for i in range(8):
            tile = held[16 * i : 16 * i + 16, 8 * p : 8 * p + 8, :].reshape(128, 128).T
            for f in range(2):
                at = 512 * p + 256 * h + 128 * f
                turned[64 * i : 64 * i + 64, at : at + 128] = tile[64 * f : 64 * f + 64, :]


def products(turned, made, out, sem, stores):
    same = lax.broadcasted_iota(jnp.int32, (128, 128), 0) == lax.broadcasted_iota(jnp.int32, (128, 128), 1)

    def scale(power):
        return lax.rsqrt(power * (LIFT**-2 / TOTAL) + 1e-06) * (1.0 / LIFT)

    def dot(a, b):
        left, right = [
            turned[256 * i : 256 * i + 256, :]
            if p is None
            else turned[256 * i : 256 * i + 256, 512 * p : 512 * p + 512]
            for i, p in (a, b)
        ]
        return lax.dot_general(left, right, (((1,), (1,)), ((), ())), preferred_element_type=jnp.float32)

    def store(p, first, count):
        at = (p, pl.ds(first, count))
        stores.append(pltpu.make_async_copy(made.at[at], out.at[at], sem.at[p, first // 256]))
        stores[-1].start()

    along, down = [], []
    for i in range(2):
        cut = slice(256 * i, 256 * i + 256)
        total = dot((i, None), (i, None))
        tiles = [jnp.where(same, total[128 * k : 128 * k + 128, 128 * k : 128 * k + 128], 0.0) for k in range(2)]
        along.append(
            scale(jnp.concatenate([jnp.sum(t, axis=0, keepdims=True) for t in tiles], axis=1)) * (1.0 / TOTAL)
        )
        down.append(scale(jnp.concatenate([jnp.sum(t, axis=1, keepdims=True) for t in tiles], axis=0)))
        made[0, cut, cut] = total * along[i] * down[i]
    mixed = dot((0, None), (1, None)) * along[1] * down[0]
    made[0, 0:256, 256:512] = mixed
    made[0, 256:512, 0:256] = mixed.T
    store(0, 0, 512)
    mixed = (dot((0, 1), (1, 0)) - dot((0, 0), (1, 1))) * along[1] * down[0]
    made[1, 0:256, 256:512] = mixed
    made[1, 256:512, 0:256] = -mixed.T
    for i in range(2):
        cut = slice(256 * i, 256 * i + 256)
        cross = dot((i, 1), (i, 0))
        made[1, cut, cut] = (cross - cross.T) * along[i] * down[i]
        store(1, 256 * i, 256)


def channelize(
    volt, window, table, out, early,
    raw, filtered, taps, whole, rows, spectra, sendbuf, held, turned, made,
    raw_sem, row_sem, send_sem, recv_sem, own_sem, in_sem, out_sem,
):
    row, column = lax.axis_index("inp"), lax.axis_index("tm")
    x, y, z, core = column // 4, row // 2, (row % 2) * 2 + (column // 2) % 2, column % 2
    me = row * 16 + column

    cuts = [(0, HALF + TAPS - 1), (HALF + TAPS - 1, FRAMES + TAPS - 1)]
    loads = []
    for h, (lo, hi) in enumerate(cuts):
        for i in range(INPUTS // 16):
            at = (pl.ds(16 * i, 16), pl.ds(lo * FRAME, (hi - lo) * FRAME))
            loads.append(pltpu.make_async_copy(volt.at[at], raw.at[at], raw_sem.at[h, i]))
    small = [
        pltpu.make_async_copy(window, taps, row_sem.at[0]),
        pltpu.make_async_copy(table, whole, row_sem.at[1]),
    ]
    for load in small[:1] + loads[:4] + small[1:] + loads[4:]:
        load.start()

    def onward(at, step):
        there = at + step
        return jnp.where(there >= 4, there - 4, there)

    xs = [onward(x, d) * 4 for d in range(4)]
    ys = [onward(y, d) * 2 for d in range(4)]
    upper = [jnp.where(onward(z, d) >= 2, 1, 0) for d in range(4)]
    lower = [(onward(z, d) - 2 * upper[d]) * 2 for d in range(4)]
    cores = [core, 1 - core]

    def chip_at(offset):
        dx, dy, dz = offset
        return ys[dy] + upper[dz], xs[dx] + lower[dz]

    barrier = pltpu.get_barrier_semaphore()
    for offset in ORDERS[0]:
        inp, tm = chip_at(offset)
        for side in range(2):
            if (offset, side) != ((0, 0, 0), 0):
                pl.semaphore_signal(barrier, inc=1, device_id=(inp, tm + cores[side]), device_id_type=MESH)
    small[0].wait()

    def exchange(j):
        h, halves, lo, count = ROUNDS[j]
        at = (pl.ds(h, halves), pl.ds(0, 127), pl.ds(lo, count))
        return pltpu.make_async_remote_copy(
            src_ref=sendbuf.at[at],
            dst_ref=out.at[at],
            send_sem=send_sem.at[j],
            recv_sem=recv_sem.at[j],
            device_id=(row, column - core + cores[1]),
            device_id_type=MESH,
        )

    def arrive(j):
        own[j].wait()
        exchange(j).wait_recv()

    own = []

    def send(j, offsets):
        h, halves, lo, count = ROUNDS[j]
        for offset in offsets:
            inp, tm = chip_at(offset)
            k = ORDERS[0].index(offset)
            for side in range(2):
                to = cores[side]
                part = sendbuf.at[pl.ds(h, halves), 2 * k + to, pl.ds(lo, count)]
                there = out.at[pl.ds(h, halves), me, pl.ds(lo, count)]
                if offset == (0, 0, 0) and side == 0:
                    copy = pltpu.make_async_copy(part, there, own_sem.at[j])
                    own.append(copy)
                else:
                    copy = pltpu.make_async_remote_copy(
                        src_ref=part,
                        dst_ref=there,
                        send_sem=send_sem.at[j],
                        recv_sem=recv_sem.at[j],
                        device_id=(inp, tm + to),
                        device_id_type=MESH,
                    )
                copy.start()

    for h in range(2):
        for i in range(INPUTS // 16):
            loads[4 * h + i].wait()

            def filter_tile(j, carry, i=i, h=h):
                at = pl.multiple_of(j * 128, 128)
                weight = [taps[pl.ds(k, 1), pl.ds(at, 128)] for k in range(TAPS)]
                held = []
                for f in range(HALF * h, HALF * h + HALF + TAPS - 1):
                    held.append(raw[pl.ds(16 * i, 16), pl.ds(f * FRAME + at, 128)].astype(jnp.float32))
                    if len(held) == TAPS:
                        total = weight[0] * held[0]
                        for k in range(1, TAPS):
                            total = total + weight[k] * held[k]
                        held.pop(0)
                        g = f - TAPS + 1
                        filtered[pl.ds(g * INPUTS + 16 * i, 16), pl.ds(at, 128)] = total.astype(jnp.bfloat16)
                return carry

            lax.fori_loop(0, FRAME // 128, filter_tile, 0)
        if h == 0:
            small[1].wait()

        for chunk in range(CHIPS // CHUNK):
            units = range(chunk * CHUNK, (chunk + 1) * CHUNK)
            if h == 0:
                for k in units:
                    inp, tm = chip_at(ORDERS[0][k])
                    at = pl.multiple_of(inp * (8 * UNIT) + tm * (UNIT // 2), UNIT)
                    rows[k * UNIT : (k + 1) * UNIT, :] = whole[pl.ds(at, UNIT), :]
            product = lax.dot_general(
                rows[chunk * ROWS : (chunk + 1) * ROWS, :],
                filtered[h * HALF * INPUTS : (h + 1) * HALF * INPUTS, :],
                (((1,), (1,)), ((), ())),
                preferred_element_type=jnp.float32,
            )
            for n in range(PAIRS):
                spectra[n * PITCH : n * PITCH + ROWS, :] = product[:, n * 128 : (n + 1) * 128]

            def gather(u, carry, chunk=chunk, h=h):
                for r in range(UNIT // 2):
                    pair = [spectra[pl.ds(u * UNIT + 2 * r + p, PAIRS, stride=PITCH), :] for p in range(2)]
                    sendbuf[h, 2 * (chunk * CHUNK + u) + r // 4, r % 4] = jnp.concatenate(pair, axis=0).astype(jnp.bfloat16)
                return carry

            lax.fori_loop(0, CHUNK, gather, 0)

            if h == 0 and chunk == 0:
                pl.semaphore_wait(barrier, 127)
            send(h, ORDERS[0][units.start : units.stop])
    send(2, ORDERS[1])

    loads = [[pltpu.make_async_copy(out.at[h, :, c], held.at[c, h], in_sem.at[c, h]) for c in range(2)] for h in range(2)]
    for h in range(2):
        arrive(h)
        for load in loads[h]:
            load.start()
        for c in range(2):
            loads[h][c].wait()
            turn(held.at[c, h], turned.at[c], h)
    stores = []
    for c in range(2):
        products(turned.at[c], made.at[c], early.at[c], out_sem.at[c], stores)
    for store in stores:
        store.wait()
    arrive(2)
    for j in range(3):
        exchange(j).wait_send()


def correlate(block, early, out, held, turned, made, passed, in_sem, out_sem, early_sem):
    loads = [
        [pltpu.make_async_copy(block.at[h, :, c + 2], held.at[c, h], in_sem.at[c, h]) for h in range(2)]
        for c in range(2)
    ]
    moves = [pltpu.make_async_copy(early.at[c], passed.at[c], early_sem.at[c]) for c in range(2)]
    for load in loads[0] + moves + loads[1]:
        load.start()
    stores = []
    for h in range(2):
        loads[0][h].wait()
        turn(held.at[0, h], turned.at[0], h)
    for c in range(2):
        moves[c].wait()
        stores.append(pltpu.make_async_copy(passed.at[c], out.at[c], early_sem.at[c]))
        stores[-1].start()
    for h in range(2):
        loads[1][h].wait()
    for h in range(2):
        turn(held.at[1, h], turned.at[1], h)
    for c in range(2):
        products(turned.at[c], made.at[c], out.at[c + 2], out_sem.at[c], stores)
    for one in stores:
        one.wait()


def on_device(volt):
    whole = pl.BlockSpec(memory_space=pl.ANY)
    work = [
        pltpu.VMEM((2, 2, 128, 16, 128), jnp.bfloat16),
        pltpu.VMEM((2, 512, 1024), jnp.bfloat16),
        pltpu.VMEM((2, 2, 512, 512), jnp.float32),
    ]
    block, early = pl.pallas_call(
        channelize,
        out_shape=[
            jax.ShapeDtypeStruct((2, 128, 4, 16, 128), jnp.bfloat16),
            jax.ShapeDtypeStruct((2, 2, 512, 512), jnp.float32),
        ],
        in_specs=[whole] * 3,
        out_specs=[whole] * 2,
        scratch_shapes=[
            pltpu.VMEM((INPUTS, (FRAMES + TAPS - 1) * FRAME), jnp.bfloat16),
            pltpu.VMEM((FRAMES * INPUTS, FRAME), jnp.bfloat16),
            pltpu.VMEM((TAPS, FRAME), jnp.float32),
            pltpu.VMEM((CHIPS * UNIT, FRAME), jnp.bfloat16),
            pltpu.VMEM((CHIPS * UNIT, FRAME), jnp.bfloat16),
            pltpu.VMEM((PAIRS * PITCH, 128), jnp.float32),
            pltpu.VMEM((2, 2 * CHIPS, 4, 16, 128), jnp.bfloat16),
            *work,
            pltpu.SemaphoreType.DMA((2, INPUTS // 16)),
            pltpu.SemaphoreType.DMA((2,)),
            pltpu.SemaphoreType.DMA((3,)),
            pltpu.SemaphoreType.DMA((3,)),
            pltpu.SemaphoreType.DMA((3,)),
            pltpu.SemaphoreType.DMA((2, 2)),
            pltpu.SemaphoreType.DMA((2, 2, 2)),
        ],
        compiler_params=pltpu.CompilerParams(
            collective_id=0, has_side_effects=True, vmem_limit_bytes=60 << 20
        ),
        name="channelize",
    )(volt, jnp.asarray(window_table()), jnp.asarray(twiddle_table()))
    return pl.pallas_call(
        correlate,
        out_shape=jax.ShapeDtypeStruct((4, 2, 512, 512), jnp.float32),
        in_specs=[whole] * 2,
        out_specs=whole,
        scratch_shapes=[
            *work,
            pltpu.VMEM((2, 2, 512, 512), jnp.float32),
            pltpu.SemaphoreType.DMA((2, 2)),
            pltpu.SemaphoreType.DMA((2, 2, 2)),
            pltpu.SemaphoreType.DMA((2,)),
        ],
        compiler_params=pltpu.CompilerParams(vmem_limit_bytes=60 << 20),
        name="correlate",
    )(block, early)


def solution(mesh):
    return jax.shard_map(
        on_device,
        mesh=mesh,
        in_specs=(P("inp", "tm"),),
        out_specs=P(("inp", "tm"), None, None, None),
        check_vma=False,
    )
```

```python
import functools
import itertools

import jax
import jax.numpy as jnp
import ml_dtypes
import numpy as np
from jax import lax
from jax.experimental import pallas as pl
from jax.experimental.pallas import tpu as pltpu
from jax.sharding import PartitionSpec as P

MESH = pl.DeviceIdType.MESH
FRAME = 1024
TAPS = 4
INPUTS = 64
FRAMES = 32
HALF = 16
PAIRS = 8
CHIPS = 64
UNIT = 16
CHUNK = 16
ROWS = CHUNK * UNIT
PITCH = ROWS + 8
TOTAL = 512
LIFT = 2.0**32


def window_table():
    index = np.arange(TAPS * FRAME, dtype=np.float64)
    shifted = (index - TAPS * FRAME / 2 + 0.5) / FRAME
    shaped = np.sinc(shifted) * (0.54 - 0.46 * np.cos(2.0 * np.pi * index / (TAPS * FRAME - 1)))
    return (shaped.reshape(TAPS, FRAME) * LIFT).astype(np.float32)


def twiddle_table():
    chans = FRAME // 2
    turn = np.arange(chans)[:, None] * np.arange(FRAME)[None, :] % FRAME
    phase = turn.astype(np.float32) * np.float32(2.0 * np.pi / FRAME)
    phase = phase.astype(np.float64)
    pair = np.stack([np.cos(phase), -np.sin(phase)], axis=1)
    return pair.reshape(2 * chans, FRAME).astype(np.float32).astype(ml_dtypes.bfloat16)


def chip_orders():
    offsets = list(itertools.product(range(4), repeat=3))[1:]
    orbits, seen = [], set()
    for start in offsets:
        if start in seen:
            continue
        orbit, now = [], start
        for _ in range(3):
            for one in (now, tuple((4 - v) % 4 for v in now)):
                if one not in orbit:
                    orbit.append(one)
            now = (now[1], now[2], now[0])
        seen.update(orbit)
        orbits.append(orbit)
    mixed = [orbits[i] for i in np.random.RandomState(1).permutation(len(orbits))]
    falling = sorted(orbits, key=lambda orbit: -sum(min(v, 4 - v) for v in orbit[0]))
    return [[o for orbit in order for o in orbit] + [(0, 0, 0)] for order in (mixed, falling)]


ORDERS = chip_orders()


ROUNDS = [(0, 1, 0, 2), (1, 1, 0, 2), (0, 2, 2, 2)]


def turn(held, turned, h):
    for p in range(2):
        for i in range(8):
            tile = held[16 * i : 16 * i + 16, 8 * p : 8 * p + 8, :].reshape(128, 128).T
            for f in range(2):
                at = 512 * p + 256 * h + 128 * f
                turned[64 * i : 64 * i + 64, at : at + 128] = tile[64 * f : 64 * f + 64, :]


def products(turned, made, out, sem, stores):
    same = lax.broadcasted_iota(jnp.int32, (128, 128), 0) == lax.broadcasted_iota(jnp.int32, (128, 128), 1)

    def scale(power):
        return lax.rsqrt(power * (LIFT**-2 / TOTAL) + 1e-06) * (1.0 / LIFT)

    def dot(a, b):
        left, right = [
            turned[256 * i : 256 * i + 256, :]
            if p is None
            else turned[256 * i : 256 * i + 256, 512 * p : 512 * p + 512]
            for i, p in (a, b)
        ]
        return lax.dot_general(left, right, (((1,), (1,)), ((), ())), preferred_element_type=jnp.float32)

    def store(p, first, count):
        at = (p, pl.ds(first, count))
        stores.append(pltpu.make_async_copy(made.at[at], out.at[at], sem.at[p, first // 256]))
        stores[-1].start()

    along, down = [], []
    for i in range(2):
        cut = slice(256 * i, 256 * i + 256)
        total = dot((i, None), (i, None))
        tiles = [jnp.where(same, total[128 * k : 128 * k + 128, 128 * k : 128 * k + 128], 0.0) for k in range(2)]
        along.append(
            scale(jnp.concatenate([jnp.sum(t, axis=0, keepdims=True) for t in tiles], axis=1)) * (1.0 / TOTAL)
        )
        down.append(scale(jnp.concatenate([jnp.sum(t, axis=1, keepdims=True) for t in tiles], axis=0)))
        made[0, cut, cut] = total * along[i] * down[i]
    mixed = dot((0, None), (1, None)) * along[1] * down[0]
    made[0, 0:256, 256:512] = mixed
    made[0, 256:512, 0:256] = mixed.T
    store(0, 0, 512)
    mixed = (dot((0, 1), (1, 0)) - dot((0, 0), (1, 1))) * along[1] * down[0]
    made[1, 0:256, 256:512] = mixed
    made[1, 256:512, 0:256] = -mixed.T
    for i in range(2):
        cut = slice(256 * i, 256 * i + 256)
        cross = dot((i, 1), (i, 0))
        made[1, cut, cut] = (cross - cross.T) * along[i] * down[i]
        store(1, 256 * i, 256)


def channelize(
    volt, window, table, out, early,
    raw, filtered, taps, whole, rows, spectra, sendbuf, held, turned, made,
    raw_sem, row_sem, send_sem, recv_sem, own_sem, in_sem, out_sem,
):
    row, column = lax.axis_index("inp"), lax.axis_index("tm")
    x, y, z, core = column // 4, row // 2, (row % 2) * 2 + (column // 2) % 2, column % 2
    me = row * 16 + column

    cuts = [(0, HALF + TAPS - 1), (HALF + TAPS - 1, FRAMES + TAPS - 1)]
    loads = []
    for h, (lo, hi) in enumerate(cuts):
        for i in range(INPUTS // 16):
            at = (pl.ds(16 * i, 16), pl.ds(lo * FRAME, (hi - lo) * FRAME))
            loads.append(pltpu.make_async_copy(volt.at[at], raw.at[at], raw_sem.at[h, i]))
    small = [
        pltpu.make_async_copy(window, taps, row_sem.at[0]),
        pltpu.make_async_copy(table, whole, row_sem.at[1]),
    ]
    for load in small[:1] + loads[:4]:
        load.start()

    def onward(at, step):
        there = at + step
        return jnp.where(there >= 4, there - 4, there)

    xs = [onward(x, d) * 4 for d in range(4)]
    ys = [onward(y, d) * 2 for d in range(4)]
    upper = [jnp.where(onward(z, d) >= 2, 1, 0) for d in range(4)]
    lower = [(onward(z, d) - 2 * upper[d]) * 2 for d in range(4)]
    cores = [core, 1 - core]

    def chip_at(offset):
        dx, dy, dz = offset
        return ys[dy] + upper[dz], xs[dx] + lower[dz]

    barrier = pltpu.get_barrier_semaphore()
    for offset in ORDERS[1]:
        inp, tm = chip_at(offset)
        for side in range(2):
            if (offset, side) != ((0, 0, 0), 0):
                pl.semaphore_signal(barrier, inc=1, device_id=(inp, tm + cores[side]), device_id_type=MESH)
    small[0].wait()

    def exchange(j):
        h, halves, lo, count = ROUNDS[j]
        at = (pl.ds(h, halves), pl.ds(0, 127), pl.ds(lo, count))
        return pltpu.make_async_remote_copy(
            src_ref=sendbuf.at[at],
            dst_ref=out.at[at],
            send_sem=send_sem.at[j],
            recv_sem=recv_sem.at[j],
            device_id=(row, column - core + cores[1]),
            device_id_type=MESH,
        )

    def arrive(j):
        own[j].wait()
        exchange(j).wait_recv()

    own = []

    def send(j, offsets):
        h, halves, lo, count = ROUNDS[j]
        for offset in offsets:
            inp, tm = chip_at(offset)
            k = ORDERS[0].index(offset)
            for side in range(2):
                to = cores[side]
                part = sendbuf.at[pl.ds(h, halves), 2 * k + to, pl.ds(lo, count)]
                there = out.at[pl.ds(h, halves), me, pl.ds(lo, count)]
                if offset == (0, 0, 0) and side == 0:
                    copy = pltpu.make_async_copy(part, there, own_sem.at[j])
                    own.append(copy)
                else:
                    copy = pltpu.make_async_remote_copy(
                        src_ref=part,
                        dst_ref=there,
                        send_sem=send_sem.at[j],
                        recv_sem=recv_sem.at[j],
                        device_id=(inp, tm + to),
                        device_id_type=MESH,
                    )
                copy.start()

    for h in range(2):
        for i in range(INPUTS // 16):
            loads[4 * h + i].wait()
            if h == 0 and i == 0:
                small[1].start()

            def filter_tile(j, carry, i=i, h=h):
                at = pl.multiple_of(j * 128, 128)
                weight = [taps[pl.ds(k, 1), pl.ds(at, 128)] for k in range(TAPS)]
                held = []
                for f in range(HALF * h, HALF * h + HALF + TAPS - 1):
                    held.append(raw[pl.ds(16 * i, 16), pl.ds(f * FRAME + at, 128)].astype(jnp.float32))
                    if len(held) == TAPS:
                        total = weight[0] * held[0]
                        for k in range(1, TAPS):
                            total = total + weight[k] * held[k]
                        held.pop(0)
                        g = f - TAPS + 1
                        filtered[pl.ds(g * INPUTS + 16 * i, 16), pl.ds(at, 128)] = total.astype(jnp.bfloat16)
                return carry

            lax.fori_loop(0, FRAME // 128, filter_tile, 0)
        if h == 0:
            for load in loads[4:]:
                load.start()
            small[1].wait()

        for chunk in range(CHIPS // CHUNK):
            units = range(chunk * CHUNK, (chunk + 1) * CHUNK)
            if h == 0:
                for k in units:
                    inp, tm = chip_at(ORDERS[0][k])
                    at = pl.multiple_of(inp * (8 * UNIT) + tm * (UNIT // 2), UNIT)
                    rows[k * UNIT : (k + 1) * UNIT, :] = whole[pl.ds(at, UNIT), :]
            product = lax.dot_general(
                rows[chunk * ROWS : (chunk + 1) * ROWS, :],
                filtered[h * HALF * INPUTS : (h + 1) * HALF * INPUTS, :],
                (((1,), (1,)), ((), ())),
                preferred_element_type=jnp.float32,
            )
            for n in range(PAIRS):
                spectra[n * PITCH : n * PITCH + ROWS, :] = product[:, n * 128 : (n + 1) * 128]

            def gather(u, carry, chunk=chunk, h=h):
                for r in range(UNIT // 2):
                    pair = [spectra[pl.ds(u * UNIT + 2 * r + p, PAIRS, stride=PITCH), :] for p in range(2)]
                    sendbuf[h, 2 * (chunk * CHUNK + u) + r // 4, r % 4] = jnp.concatenate(pair, axis=0).astype(jnp.bfloat16)
                return carry

            lax.fori_loop(0, CHUNK, gather, 0)

            if h == 0 and chunk == 0:
                pl.semaphore_wait(barrier, 127)
            send(h, ORDERS[0][units.start : units.stop])
    send(2, ORDERS[1])

    loads = [[pltpu.make_async_copy(out.at[h, :, c], held.at[c, h], in_sem.at[c, h]) for c in range(2)] for h in range(2)]
    for h in range(2):
        arrive(h)
        for load in loads[h]:
            load.start()
        for c in range(2):
            loads[h][c].wait()
            turn(held.at[c, h], turned.at[c], h)
    stores = []
    for c in range(2):
        products(turned.at[c], made.at[c], early.at[c], out_sem.at[c], stores)
    for store in stores:
        store.wait()
    arrive(2)
    for j in range(3):
        exchange(j).wait_send()


def correlate(block, early, out, held, turned, made, passed, in_sem, out_sem, early_sem):
    loads = [
        [pltpu.make_async_copy(block.at[h, :, c + 2], held.at[c, h], in_sem.at[c, h]) for h in range(2)]
        for c in range(2)
    ]
    moves = [pltpu.make_async_copy(early.at[c], passed.at[c], early_sem.at[c]) for c in range(2)]
    for load in moves + loads[0] + loads[1]:
        load.start()
    stores = []
    for h in range(2):
        loads[0][h].wait()
        turn(held.at[0, h], turned.at[0], h)
    for c in range(2):
        moves[c].wait()
        stores.append(pltpu.make_async_copy(passed.at[c], out.at[c], early_sem.at[c]))
        stores[-1].start()
    for h in range(2):
        loads[1][h].wait()
    for h in range(2):
        turn(held.at[1, h], turned.at[1], h)
    for c in range(2):
        products(turned.at[c], made.at[c], out.at[c + 2], out_sem.at[c], stores)
    for one in stores:
        one.wait()


def on_device(volt):
    whole = pl.BlockSpec(memory_space=pl.ANY)
    work = [
        pltpu.VMEM((2, 2, 128, 16, 128), jnp.bfloat16),
        pltpu.VMEM((2, 512, 1024), jnp.bfloat16),
        pltpu.VMEM((2, 2, 512, 512), jnp.float32),
    ]
    block, early = pl.pallas_call(
        channelize,
        out_shape=[
            jax.ShapeDtypeStruct((2, 128, 4, 16, 128), jnp.bfloat16),
            jax.ShapeDtypeStruct((2, 2, 512, 512), jnp.float32),
        ],
        in_specs=[whole] * 3,
        out_specs=[whole] * 2,
        scratch_shapes=[
            pltpu.VMEM((INPUTS, (FRAMES + TAPS - 1) * FRAME), jnp.bfloat16),
            pltpu.VMEM((FRAMES * INPUTS, FRAME), jnp.bfloat16),
            pltpu.VMEM((TAPS, FRAME), jnp.float32),
            pltpu.VMEM((CHIPS * UNIT, FRAME), jnp.bfloat16),
            pltpu.VMEM((CHIPS * UNIT, FRAME), jnp.bfloat16),
            pltpu.VMEM((PAIRS * PITCH, 128), jnp.float32),
            pltpu.VMEM((2, 2 * CHIPS, 4, 16, 128), jnp.bfloat16),
            *work,
            pltpu.SemaphoreType.DMA((2, INPUTS // 16)),
            pltpu.SemaphoreType.DMA((2,)),
            pltpu.SemaphoreType.DMA((3,)),
            pltpu.SemaphoreType.DMA((3,)),
            pltpu.SemaphoreType.DMA((3,)),
            pltpu.SemaphoreType.DMA((2, 2)),
            pltpu.SemaphoreType.DMA((2, 2, 2)),
        ],
        compiler_params=pltpu.CompilerParams(
            collective_id=0, has_side_effects=True, vmem_limit_bytes=60 << 20
        ),
        name="channelize",
    )(volt, jnp.asarray(window_table()), jnp.asarray(twiddle_table()))
    return pl.pallas_call(
        correlate,
        out_shape=jax.ShapeDtypeStruct((4, 2, 512, 512), jnp.float32),
        in_specs=[whole] * 2,
        out_specs=whole,
        scratch_shapes=[
            *work,
            pltpu.VMEM((2, 2, 512, 512), jnp.float32),
            pltpu.SemaphoreType.DMA((2, 2)),
            pltpu.SemaphoreType.DMA((2, 2, 2)),
            pltpu.SemaphoreType.DMA((2,)),
        ],
        compiler_params=pltpu.CompilerParams(vmem_limit_bytes=60 << 20),
        name="correlate",
    )(block, early)


def solution(mesh):
    return jax.shard_map(
        on_device,
        mesh=mesh,
        in_specs=(P("inp", "tm"),),
        out_specs=P(("inp", "tm"), None, None, None),
        check_vma=False,
    )
```

```python
import functools
import itertools

import jax
import jax.numpy as jnp
import ml_dtypes
import numpy as np
from jax import lax
from jax.experimental import pallas as pl
from jax.experimental.pallas import tpu as pltpu
from jax.sharding import PartitionSpec as P

MESH = pl.DeviceIdType.MESH
FRAME = 1024
TAPS = 4
INPUTS = 64
FRAMES = 32
HALF = 16
PAIRS = 8
CHIPS = 64
UNIT = 16
CHUNK = 8
ROWS = CHUNK * UNIT
PITCH = ROWS + 8
TOTAL = 512
LIFT = 2.0**32


def window_table():
    index = np.arange(TAPS * FRAME, dtype=np.float64)
    shifted = (index - TAPS * FRAME / 2 + 0.5) / FRAME
    shaped = np.sinc(shifted) * (0.54 - 0.46 * np.cos(2.0 * np.pi * index / (TAPS * FRAME - 1)))
    return (shaped.reshape(TAPS, FRAME) * LIFT).astype(np.float32)


def twiddle_table():
    chans = FRAME // 2
    turn = np.arange(chans)[:, None] * np.arange(FRAME)[None, :] % FRAME
    phase = turn.astype(np.float32) * np.float32(2.0 * np.pi / FRAME)
    phase = phase.astype(np.float64)
    pair = np.stack([np.cos(phase), -np.sin(phase)], axis=1)
    return pair.reshape(2 * chans, FRAME).astype(np.float32).astype(ml_dtypes.bfloat16)


def chip_orders():
    offsets = list(itertools.product(range(4), repeat=3))[1:]
    orbits, seen = [], set()
    for start in offsets:
        if start in seen:
            continue
        orbit, now = [], start
        for _ in range(3):
            for one in (now, tuple((4 - v) % 4 for v in now)):
                if one not in orbit:
                    orbit.append(one)
            now = (now[1], now[2], now[0])
        seen.update(orbit)
        orbits.append(orbit)
    mixed = [orbits[i] for i in np.random.RandomState(1).permutation(len(orbits))]
    falling = sorted(orbits, key=lambda orbit: -sum(min(v, 4 - v) for v in orbit[0]))
    return [[o for orbit in order for o in orbit] + [(0, 0, 0)] for order in (mixed, falling)]


ORDERS = chip_orders()


ROUNDS = [(0, 1, 0, 2), (1, 1, 0, 2), (0, 2, 2, 2)]


def turn(held, turned, h):
    for p in range(2):
        for i in range(8):
            tile = held[16 * i : 16 * i + 16, 8 * p : 8 * p + 8, :].reshape(128, 128).T
            for f in range(2):
                at = 512 * p + 256 * h + 128 * f
                turned[64 * i : 64 * i + 64, at : at + 128] = tile[64 * f : 64 * f + 64, :]


def products(turned, made, out, sem, stores):
    same = lax.broadcasted_iota(jnp.int32, (128, 128), 0) == lax.broadcasted_iota(jnp.int32, (128, 128), 1)

    def scale(power):
        return lax.rsqrt(power * (LIFT**-2 / TOTAL) + 1e-06) * (1.0 / LIFT)

    def dot(a, b):
        left, right = [
            turned[256 * i : 256 * i + 256, :]
            if p is None
            else turned[256 * i : 256 * i + 256, 512 * p : 512 * p + 512]
            for i, p in (a, b)
        ]
        return lax.dot_general(left, right, (((1,), (1,)), ((), ())), preferred_element_type=jnp.float32)

    def store(p, first, count):
        at = (p, pl.ds(first, count))
        stores.append(pltpu.make_async_copy(made.at[at], out.at[at], sem.at[p, first // 256]))
        stores[-1].start()

    along, down = [], []
    for i in range(2):
        cut = slice(256 * i, 256 * i + 256)
        total = dot((i, None), (i, None))
        tiles = [jnp.where(same, total[128 * k : 128 * k + 128, 128 * k : 128 * k + 128], 0.0) for k in range(2)]
        along.append(
            scale(jnp.concatenate([jnp.sum(t, axis=0, keepdims=True) for t in tiles], axis=1)) * (1.0 / TOTAL)
        )
        down.append(scale(jnp.concatenate([jnp.sum(t, axis=1, keepdims=True) for t in tiles], axis=0)))
        made[0, cut, cut] = total * along[i] * down[i]
    mixed = dot((0, None), (1, None)) * along[1] * down[0]
    made[0, 0:256, 256:512] = mixed
    made[0, 256:512, 0:256] = mixed.T
    store(0, 0, 512)
    mixed = (dot((0, 1), (1, 0)) - dot((0, 0), (1, 1))) * along[1] * down[0]
    made[1, 0:256, 256:512] = mixed
    made[1, 256:512, 0:256] = -mixed.T
    for i in range(2):
        cut = slice(256 * i, 256 * i + 256)
        cross = dot((i, 1), (i, 0))
        made[1, cut, cut] = (cross - cross.T) * along[i] * down[i]
        store(1, 256 * i, 256)


def channelize(
    volt, window, table, out, early,
    raw, filtered, taps, whole, rows, spectra, sendbuf, held, turned, made,
    raw_sem, row_sem, send_sem, recv_sem, own_sem, in_sem, out_sem,
):
    row, column = lax.axis_index("inp"), lax.axis_index("tm")
    x, y, z, core = column // 4, row // 2, (row % 2) * 2 + (column // 2) % 2, column % 2
    me = row * 16 + column

    cuts = [(0, HALF + TAPS - 1), (HALF + TAPS - 1, FRAMES + TAPS - 1)]
    loads = []
    for h, (lo, hi) in enumerate(cuts):
        for i in range(INPUTS // 16):
            at = (pl.ds(16 * i, 16), pl.ds(lo * FRAME, (hi - lo) * FRAME))
            loads.append(pltpu.make_async_copy(volt.at[at], raw.at[at], raw_sem.at[h, i]))
    small = [
        pltpu.make_async_copy(window, taps, row_sem.at[0]),
        pltpu.make_async_copy(table, whole, row_sem.at[1]),
    ]
    for load in small[:1] + loads[:4]:
        load.start()

    def onward(at, step):
        there = at + step
        return jnp.where(there >= 4, there - 4, there)

    xs = [onward(x, d) * 4 for d in range(4)]
    ys = [onward(y, d) * 2 for d in range(4)]
    upper = [jnp.where(onward(z, d) >= 2, 1, 0) for d in range(4)]
    lower = [(onward(z, d) - 2 * upper[d]) * 2 for d in range(4)]
    cores = [core, 1 - core]

    def chip_at(offset):
        dx, dy, dz = offset
        return ys[dy] + upper[dz], xs[dx] + lower[dz]

    barrier = pltpu.get_barrier_semaphore()
    for offset in ORDERS[1]:
        inp, tm = chip_at(offset)
        for side in range(2):
            if (offset, side) != ((0, 0, 0), 0):
                pl.semaphore_signal(barrier, inc=1, device_id=(inp, tm + cores[side]), device_id_type=MESH)
    small[0].wait()

    def exchange(j):
        h, halves, lo, count = ROUNDS[j]
        at = (pl.ds(h, halves), pl.ds(0, 127), pl.ds(lo, count))
        return pltpu.make_async_remote_copy(
            src_ref=sendbuf.at[at],
            dst_ref=out.at[at],
            send_sem=send_sem.at[j],
            recv_sem=recv_sem.at[j],
            device_id=(row, column - core + cores[1]),
            device_id_type=MESH,
        )

    def arrive(j):
        own[j].wait()
        exchange(j).wait_recv()

    own = []

    def send(j, offsets):
        h, halves, lo, count = ROUNDS[j]
        for offset in offsets:
            inp, tm = chip_at(offset)
            k = ORDERS[0].index(offset)
            for side in range(2):
                to = cores[side]
                part = sendbuf.at[pl.ds(h, halves), 2 * k + to, pl.ds(lo, count)]
                there = out.at[pl.ds(h, halves), me, pl.ds(lo, count)]
                if offset == (0, 0, 0) and side == 0:
                    copy = pltpu.make_async_copy(part, there, own_sem.at[j])
                    own.append(copy)
                else:
                    copy = pltpu.make_async_remote_copy(
                        src_ref=part,
                        dst_ref=there,
                        send_sem=send_sem.at[j],
                        recv_sem=recv_sem.at[j],
                        device_id=(inp, tm + to),
                        device_id_type=MESH,
                    )
                copy.start()

    for h in range(2):
        for i in range(INPUTS // 16):
            loads[4 * h + i].wait()
            if h == 0 and i == 0:
                small[1].start()

            def filter_tile(j, carry, i=i, h=h):
                at = pl.multiple_of(j * 128, 128)
                weight = [taps[pl.ds(k, 1), pl.ds(at, 128)] for k in range(TAPS)]
                held = []
                for f in range(HALF * h, HALF * h + HALF + TAPS - 1):
                    held.append(raw[pl.ds(16 * i, 16), pl.ds(f * FRAME + at, 128)].astype(jnp.float32))
                    if len(held) == TAPS:
                        total = weight[0] * held[0]
                        for k in range(1, TAPS):
                            total = total + weight[k] * held[k]
                        held.pop(0)
                        g = f - TAPS + 1
                        filtered[pl.ds(g * INPUTS + 16 * i, 16), pl.ds(at, 128)] = total.astype(jnp.bfloat16)
                return carry

            lax.fori_loop(0, FRAME // 128, filter_tile, 0)
        if h == 0:
            for load in loads[4:]:
                load.start()
            small[1].wait()

        for chunk in range(CHIPS // CHUNK):
            units = range(chunk * CHUNK, (chunk + 1) * CHUNK)
            if h == 0:
                for k in units:
                    inp, tm = chip_at(ORDERS[0][k])
                    at = pl.multiple_of(inp * (8 * UNIT) + tm * (UNIT // 2), UNIT)
                    rows[k * UNIT : (k + 1) * UNIT, :] = whole[pl.ds(at, UNIT), :]
            product = lax.dot_general(
                rows[chunk * ROWS : (chunk + 1) * ROWS, :],
                filtered[h * HALF * INPUTS : (h + 1) * HALF * INPUTS, :],
                (((1,), (1,)), ((), ())),
                preferred_element_type=jnp.float32,
            )
            for n in range(PAIRS):
                spectra[n * PITCH : n * PITCH + ROWS, :] = product[:, n * 128 : (n + 1) * 128]

            def gather(u, carry, chunk=chunk, h=h):
                for r in range(UNIT // 2):
                    pair = [spectra[pl.ds(u * UNIT + 2 * r + p, PAIRS, stride=PITCH), :] for p in range(2)]
                    sendbuf[h, 2 * (chunk * CHUNK + u) + r // 4, r % 4] = jnp.concatenate(pair, axis=0).astype(jnp.bfloat16)
                return carry

            lax.fori_loop(0, CHUNK, gather, 0)

            if h == 0 and chunk == 0:
                pl.semaphore_wait(barrier, 127)
            send(h, ORDERS[0][units.start : units.stop])
    send(2, ORDERS[1])

    loads = [[pltpu.make_async_copy(out.at[h, :, c], held.at[c, h], in_sem.at[c, h]) for c in range(2)] for h in range(2)]
    for h in range(2):
        arrive(h)
        for load in loads[h]:
            load.start()
        for c in range(2):
            loads[h][c].wait()
            turn(held.at[c, h], turned.at[c], h)
    stores = []
    for c in range(2):
        products(turned.at[c], made.at[c], early.at[c], out_sem.at[c], stores)
    for store in stores:
        store.wait()
    arrive(2)
    for j in range(3):
        exchange(j).wait_send()


def correlate(block, early, out, held, turned, made, passed, in_sem, out_sem, early_sem):
    loads = [
        [pltpu.make_async_copy(block.at[h, :, c + 2], held.at[c, h], in_sem.at[c, h]) for h in range(2)]
        for c in range(2)
    ]
    moves = [pltpu.make_async_copy(early.at[c], passed.at[c], early_sem.at[c]) for c in range(2)]
    for load in moves + loads[0] + loads[1]:
        load.start()
    stores = []
    for h in range(2):
        loads[0][h].wait()
        turn(held.at[0, h], turned.at[0], h)
    for c in range(2):
        moves[c].wait()
        stores.append(pltpu.make_async_copy(passed.at[c], out.at[c], early_sem.at[c]))
        stores[-1].start()
    for h in range(2):
        loads[1][h].wait()
    for h in range(2):
        turn(held.at[1, h], turned.at[1], h)
    for c in range(2):
        products(turned.at[c], made.at[c], out.at[c + 2], out_sem.at[c], stores)
    for one in stores:
        one.wait()


def on_device(volt):
    whole = pl.BlockSpec(memory_space=pl.ANY)
    work = [
        pltpu.VMEM((2, 2, 128, 16, 128), jnp.bfloat16),
        pltpu.VMEM((2, 512, 1024), jnp.bfloat16),
        pltpu.VMEM((2, 2, 512, 512), jnp.float32),
    ]
    block, early = pl.pallas_call(
        channelize,
        out_shape=[
            jax.ShapeDtypeStruct((2, 128, 4, 16, 128), jnp.bfloat16),
            jax.ShapeDtypeStruct((2, 2, 512, 512), jnp.float32),
        ],
        in_specs=[whole] * 3,
        out_specs=[whole] * 2,
        scratch_shapes=[
            pltpu.VMEM((INPUTS, (FRAMES + TAPS - 1) * FRAME), jnp.bfloat16),
            pltpu.VMEM((FRAMES * INPUTS, FRAME), jnp.bfloat16),
            pltpu.VMEM((TAPS, FRAME), jnp.float32),
            pltpu.VMEM((CHIPS * UNIT, FRAME), jnp.bfloat16),
            pltpu.VMEM((CHIPS * UNIT, FRAME), jnp.bfloat16),
            pltpu.VMEM((PAIRS * PITCH, 128), jnp.float32),
            pltpu.VMEM((2, 2 * CHIPS, 4, 16, 128), jnp.bfloat16),
            *work,
            pltpu.SemaphoreType.DMA((2, INPUTS // 16)),
            pltpu.SemaphoreType.DMA((2,)),
            pltpu.SemaphoreType.DMA((3,)),
            pltpu.SemaphoreType.DMA((3,)),
            pltpu.SemaphoreType.DMA((3,)),
            pltpu.SemaphoreType.DMA((2, 2)),
            pltpu.SemaphoreType.DMA((2, 2, 2)),
        ],
        compiler_params=pltpu.CompilerParams(
            collective_id=0, has_side_effects=True, vmem_limit_bytes=60 << 20
        ),
        name="channelize",
    )(volt, jnp.asarray(window_table()), jnp.asarray(twiddle_table()))
    return pl.pallas_call(
        correlate,
        out_shape=jax.ShapeDtypeStruct((4, 2, 512, 512), jnp.float32),
        in_specs=[whole] * 2,
        out_specs=whole,
        scratch_shapes=[
            *work,
            pltpu.VMEM((2, 2, 512, 512), jnp.float32),
            pltpu.SemaphoreType.DMA((2, 2)),
            pltpu.SemaphoreType.DMA((2, 2, 2)),
            pltpu.SemaphoreType.DMA((2,)),
        ],
        compiler_params=pltpu.CompilerParams(vmem_limit_bytes=60 << 20),
        name="correlate",
    )(block, early)


def solution(mesh):
    return jax.shard_map(
        on_device,
        mesh=mesh,
        in_specs=(P("inp", "tm"),),
        out_specs=P(("inp", "tm"), None, None, None),
        check_vma=False,
    )
```
